128 devices in a mesh: row: 16 (over x, z), col: 8 (over y, core).
Axes of the slice: x: 4, y: 4, z: 4, core: 2. Of those that a mesh axis runs over, the one named last changes fastest.
Arguments:
- working: float32 [16384, 16384], P('row', 'col'), as said below
- step: int32 [1], replicated, may hold values from 0 to 122
Outputs:
- factored: float32 [16384, 16384], P('row', 'col')
The draws below stay inside these ranges and needn't reach their ends.
Inputs may be any that keep to these rules, and one draw needn't show every extreme that they name: working is symmetric positive definite: a Matern covariance (smoothness 3/2) of sites on a grid, with scaled rows and a positive nugget on the diagonal.
All inputs are finite; a program needn't handle non-finite values.
Results may differ from the reference program's by a relative error of at most 0.0001.
Values sent between devices are 32-bit elements; how exact they have to be, the bound alone decides.
A program may use at most 128 MiB of HBM per device.

```python
import jax
import jax.numpy as jnp
from jax import lax

B = 128
TR = 8
STEPS = 6
TC = 16
NT = 128
M = 16384
N_ROW = 16
N_COL = 8


def draw_working(key, part):
    key = jax.random.fold_in(key, 11)
    key_sites, key_scale, key_nugget = jax.random.split(key, 3)
    cells = M // 64 * 128
    sites = jax.random.permutation(key_sites, cells)[:M]
    coord_x = (sites // 128).astype(jnp.float32)
    coord_y = (sites % 128).astype(jnp.float32)
    scale = jnp.exp(jax.random.uniform(key_scale, (M,), jnp.float32, jnp.log(0.5), jnp.log(3.0)))
    nugget = jax.random.uniform(key_nugget, (M,), jnp.float32, 0.3, 1.0)
    reach = 1.0 / 24.0
    delta_x = coord_x[:, None] - coord_x[None, :]
    delta_y = coord_y[:, None] - coord_y[None, :]
    radius = jnp.sqrt(delta_x * delta_x + delta_y * delta_y) * (reach * 1.7320508)
    kernel = (1.0 + radius) * jnp.exp(-radius)
    whole = scale[:, None] * scale[None, :] * kernel + jnp.diag(scale * scale * nugget)
    return whole.reshape(TR, N_ROW, B, TC, N_COL, B).transpose(1, 0, 2, 4, 3, 5).reshape(M, M).astype(jnp.float32)


def setup_inputs(seed: int = 0) -> dict:
    streams_of = jax.random.split(jax.random.key(seed), 3)
    working = draw_working(jax.random.fold_in(streams_of[2], 71), 0)
    step = jax.random.randint(streams_of[1], (1,), 0, NT - STEPS + 1).astype(jnp.int32)
    return dict(working=working, step=step)


def to_global(stored):
    return stored.reshape(N_ROW, TR, B, N_COL, TC, B).transpose(1, 0, 2, 4, 3, 5).reshape(M, M)

def from_global(whole):
    return whole.reshape(TR, N_ROW, B, TC, N_COL, B).transpose(1, 0, 2, 4, 3, 5).reshape(M, M)

def reference(working, step):
    whole = to_global(working)
    start = step[0].astype(jnp.int32)
    tile_of = (jnp.arange(M) // B).astype(jnp.int32)
    for turn in range(STEPS):
        k = start + turn
        diag = lax.dynamic_slice(whole, (k * B, k * B), (B, B))
        factor = jnp.linalg.cholesky(diag)
        column = lax.dynamic_slice_in_dim(whole, k * B, B, 1)
        solved = lax.linalg.triangular_solve(factor, column, left_side=False, lower=True, transpose_a=True)
        panel = jnp.where((tile_of > k)[:, None], solved, 0.0)

        def row_block(index, current):
            index = index.astype(jnp.int32)
            rows = lax.dynamic_slice_in_dim(panel, index * B, B, 0)
            update = jnp.dot(rows, panel.T, precision=lax.Precision.HIGHEST)
            keep = (index >= tile_of)[None, :]
            block = lax.dynamic_slice_in_dim(current, index * B, B, 0)
            return lax.dynamic_update_slice_in_dim(current, block - jnp.where(keep, update, 0.0), index * B, 0)
        whole = lax.fori_loop(0, M // B, row_block, whole)
        stacked = jnp.tile(factor, (M // B, 1))
        new_column = jnp.where((tile_of > k)[:, None], solved, jnp.where((tile_of == k)[:, None], stacked, column))
        whole = lax.dynamic_update_slice_in_dim(whole, new_column, k * B, 1)
    return from_global(whole)
```

```python
import functools

import jax
import jax.numpy as jnp
from jax import lax
from jax.experimental import pallas as pl
from jax.experimental.pallas import tpu as pltpu
from jax.sharding import PartitionSpec as P

B = 128
STEPS = 6
W = B * STEPS
F32 = jnp.float32
BF16 = jnp.bfloat16
MESH = pl.DeviceIdType.MESH
HIGHEST = lax.Precision.HIGHEST
NT = (((1,), (1,)), ((), ()))
NN = (((1,), (0,)), ((), ()))


def factor_tile(tile):
    chunk = 8
    rest = tile
    other = (
        lax.broadcasted_iota(jnp.int32, (B, B), 0) == lax.broadcasted_iota(jnp.int32, (B, B), 1)
    ).astype(F32)
    uppers, inverses = [], []
    for first in range(0, B, chunk):
        rows = B - first
        row = lax.broadcasted_iota(jnp.int32, (rows, B), 0)
        coefs = [
            jnp.broadcast_to(rest[:, first + i : first + i + 1], (rows, B)) for i in range(chunk)
        ]
        scales = []
        for j in range(chunk):
            scale = lax.rsqrt(coefs[j][j : j + 1, :])
            scales.append(scale)
            factor = jnp.where(row > j, coefs[j] * (scale * scale), 0.0)
            rest = rest - factor * rest[j : j + 1, :]
            other = other - factor * other[j : j + 1, :]
            for i in range(j + 1, chunk):
                coefs[i] = coefs[i] - factor * coefs[i][j : j + 1, :]
        scale = jnp.concatenate(scales, 0)
        sub = lax.broadcasted_iota(jnp.int32, (chunk, B), 0)
        lane = lax.broadcasted_iota(jnp.int32, (chunk, B), 1)
        uppers.append(jnp.where(lane >= first + sub, rest[:chunk] * scale, 0.0))
        inverses.append(other[:chunk] * scale)
        rest, other = rest[chunk:], other[chunk:]
    return jnp.concatenate(uppers, 0), jnp.concatenate(inverses, 0)


class Ring:
    MESSAGES = (
        (
            ((0, 0), None, (1, 0)),
            ((0, 0), None, (-1, 0)),
            ((0, 0), None, (0, 1)),
            ((0, 0), None, (0, -1)),
        ),
        (
            ((-1, 0), 0, (1, 0)),
            ((1, 0), 1, (-1, 0)),
            ((0, -1), 0, (0, 1)),
            ((0, 1), 1, (0, -1)),
            ((-1, 0), None, (0, 1)),
            ((-1, 0), None, (0, -1)),
            ((1, 0), None, (0, 1)),
            ((1, 0), None, (0, -1)),
        ),
        (
            ((2, 0), None, (0, 1)),
            ((2, 0), None, (0, -1)),
            ((-1, -1), 0, (0, 1)),
            ((1, -1), 0, (0, 1)),
            ((-1, 1), 1, (0, -1)),
            ((1, 1), 1, (0, -1)),
        ),
        (
            ((2, -1), 0, (0, 1)),
            ((2, 1), 1, (0, -1)),
        ),
    )
    COUNT = 20

    def __init__(self, row, col, view, own, send_sem, recv_sem):
        core = lax.rem(col, 2)
        x, z = row // 4, lax.rem(row, 4)
        self.u = z + core * (x - z)
        self.v = x + core * (z - x)
        self.su, self.sv = 1 + 3 * core, 4 - 3 * core
        self.col, self.view, self.own = col, view, own
        self.send_sem, self.recv_sem = send_sem, recv_sem

    def index(self, du, dv):
        return self.su * lax.rem(self.u + du + 4, 4) + self.sv * lax.rem(self.v + dv + 4, 4)

    def copy(self, number, message, receiving):
        (du, dv), part, (au, av) = message
        if receiving:
            du, dv = du - au, dv - av
        block = self.index(du, dv)
        dst = self.view(block, part)
        src = self.own if (du, dv) == (0, 0) and not receiving and self.own is not None else dst
        return pltpu.make_async_remote_copy(
            src_ref=src,
            dst_ref=dst,
            send_sem=self.send_sem.at[number],
            recv_sem=self.recv_sem.at[number],
            device_id=(self.index(au, av), self.col),
            device_id_type=MESH,
        )

    def numbered(self, tick):
        base = sum(len(m) for m in self.MESSAGES[:tick])
        return [(base + i, m) for i, m in enumerate(self.MESSAGES[tick])]

    def tick(self, tick):
        if tick > 0:
            for number, message in self.numbered(tick - 1):
                self.copy(number, message, True).wait_recv()
        if tick < len(self.MESSAGES):
            for number, message in self.numbered(tick):
                self.copy(number, message, False).start()

    def finish(self):
        for tick in range(len(self.MESSAGES)):
            for number, message in self.numbered(tick):
                self.copy(number, message, False).wait_send()


def gather_kernel(
    idx, tile, strip, slab,
    upper_o, inverse_o, lower_o, rout, cout,
    dbuf, dcol, dcg, whole, rbuf, bst,
    d1s, d1r, a1s, a1r, d2s, d2r, d3s, d3r, sibs, sibr, rs, rr, cs, cr, local,
):
    p, q = lax.axis_index("row"), lax.axis_index("col")
    core, y = lax.rem(q, 2), q // 2
    sibling = q + 1 - 2 * core

    barrier = pltpu.get_barrier_semaphore()
    for d in range(1, 16):
        pl.semaphore_signal(barrier, inc=1, device_id=(lax.rem(p + d, 16), q), device_id_type=MESH)
    for d in range(1, 8):
        pl.semaphore_signal(barrier, inc=1, device_id=(p, lax.rem(q + d, 8)), device_id_type=MESH)
    pl.semaphore_wait(barrier, 22)

    def remote(src, dst, send, recv, device):
        return pltpu.make_async_remote_copy(
            src_ref=src, dst_ref=dst, send_sem=send, recv_sem=recv,
            device_id=device, device_id_type=MESH,
        )

    def diag(d, slot):
        to = lax.rem(p + d, 16)
        rows = pl.ds(pl.multiple_of(8 * to, 8), 8)
        return remote(tile.at[rows, :], dbuf.at[slot], d1s.at[d], d1r.at[d], (to, q))

    def piece(d, slot):
        to = lax.rem(p + d, 16)
        columns = pl.ds(pl.multiple_of(B * to, B), B)
        return remote(strip.at[:, columns], rbuf.at[slot], a1s.at[d], a1r.at[d], (to, q))

    def spread(d, slot):
        to = lax.rem(q + d, 8)
        return remote(dcol, dcg.at[slot], d2s.at[d], d2r.at[d], (p, to))

    for d in range(1, 16):
        diag(d, p).start()
    for d in range(1, 16):
        piece(d, p).start()
    own_piece = pltpu.make_async_copy(
        strip.at[:, pl.ds(pl.multiple_of(B * p, B), B)], rbuf.at[p], local.at[0]
    )
    own_piece.start()
    own_slab = pltpu.make_async_copy(slab, cout.at[q], local.at[1])
    own_slab.start()
    dbuf[p] = tile[pl.ds(pl.multiple_of(8 * p, 8), 8), :]
    for d in range(1, 16):
        diag(d, lax.rem(p + 16 - d, 16)).wait_recv()
    for s in range(STEPS):
        block = dbuf[idx[s]]
        dcol[s] = block
        dcg[q, s] = block
    for d in range(1, 8):
        spread(d, q).start()

    def slot(dy):
        return lax.rem(y + dy + 4, 4) * 2 + core

    def part_of(block, part):
        return cout.at[block] if part is None else cout.at[block, pl.ds(512 * part, 512), :]

    def along(n, dy, part, ay, receiving):
        block = slot(dy - ay if receiving else dy)
        dst = part_of(block, part)
        src = slab if dy == 0 and not receiving else dst
        return remote(src, dst, cs.at[n], cr.at[n], (p, slot(ay)))

    def across(n, dy, receiving):
        block = slot(dy) + 1 - 2 * core if receiving else slot(dy)
        src = slab if dy == 0 and not receiving else cout.at[block]
        return remote(src, cout.at[block], cs.at[n], cr.at[n], (p, sibling))

    along_messages = ((0, 0, None, 1), (1, 0, None, -1), (3, -1, 0, 1), (4, 1, 1, -1))
    across_messages = ((2, 0), (5, -1), (6, 1), (7, 2))

    def columns_tick(tick):
        if tick == 0:
            along(*along_messages[0], False).start()
            along(*along_messages[1], False).start()
            across(*across_messages[0], False).start()
        elif tick == 1:
            along(*along_messages[0], True).wait_recv()
            along(*along_messages[1], True).wait_recv()
            along(*along_messages[2], False).start()
            along(*along_messages[3], False).start()
            across(*across_messages[1], False).start()
            across(*across_messages[2], False).start()
        elif tick == 2:
            along(*along_messages[2], True).wait_recv()
            along(*along_messages[3], True).wait_recv()
            across(*across_messages[3], False).start()
        else:
            for message in across_messages:
                across(*message, True).wait_recv()
            for message in along_messages:
                along(*message, False).wait_send()
            for message in across_messages:
                across(*message, False).wait_send()

    for d in range(1, 8):
        spread(d, lax.rem(q + 8 - d, 8)).wait_recv()
    half = pl.ds(3 * core, 3)
    for b in range(STEPS):
        whole[half, p, :, b * B : (b + 1) * B] = dcg[idx[STEPS + b], half]

    def diag_view(block, part):
        if part is None:
            return whole.at[half, block]
        return whole.at[half, block, :, pl.ds(384 * part, 384)]

    def row_view(block, part):
        return rout.at[block] if part is None else rout.at[block, pl.ds(384 * part, 384), :]

    diag_ring = Ring(p, q, diag_view, None, d3s, d3r)
    row_ring = Ring(p, q, row_view, bst, rs, rr)
    diag_ring.tick(0)
    columns_tick(0)

    own_piece.wait()
    for d in range(1, 16):
        piece(d, lax.rem(p + 16 - d, 16)).wait_recv()
    for s in range(STEPS):
        bst[s * B : (s + 1) * B, :] = rbuf[idx[s]]
    own_rows = pltpu.make_async_copy(bst, rout.at[p], local.at[2])
    own_rows.start()
    diag_ring.tick(1)
    diag_ring.tick(2)
    diag_ring.tick(3)
    row_ring.tick(0)
    diag_ring.tick(4)
    other = pl.ds(3 - 3 * core, 3)
    to_sibling = remote(whole.at[half], whole.at[half], sibs, sibr, (p, sibling))
    from_sibling = remote(whole.at[other], whole.at[other], sibs, sibr, (p, sibling))
    to_sibling.start()
    columns_tick(1)
    from_sibling.wait_recv()
    to_sibling.wait_send()
    diag_ring.finish()

    def step(k, carry):
        here = pl.ds(pl.multiple_of(k * B, B), B)
        upper, inverse = factor_tile(whole[k, :, :, here].reshape(B, B))
        upper_o[k] = upper
        inverse_o[k] = inverse
        for i in range(STEPS):

            @pl.when(k == i)
            def _():
                if i < STEPS - 1:
                    left = STEPS - 1 - i
                    below = whole[i + 1 :, :, :, i * B : (i + 1) * B].reshape(left * B, B)
                    solved = lax.dot_general(
                        below, inverse_o[i], NT, precision=HIGHEST, preferred_element_type=F32
                    )
                    lower_o[i, (i + 1) * B :, :] = solved
                    update = lax.dot_general(
                        solved, solved, NT, precision=HIGHEST, preferred_element_type=F32
                    )
                    whole[i + 1 :, :, :, (i + 1) * B :] = whole[
                        i + 1 :, :, :, (i + 1) * B :
                    ] - update.reshape(left, 16, 8, left * B)
                if i == 0:
                    row_ring.tick(1)
                    columns_tick(2)
                if i == 2:
                    row_ring.tick(2)
                if i == 4:
                    row_ring.tick(3)
                if i == 5:
                    row_ring.tick(4)

        return carry

    lax.fori_loop(0, STEPS, step, 0)
    columns_tick(3)
    row_ring.finish()
    for d in range(1, 16):
        diag(d, p).wait_send()
        piece(d, p).wait_send()
    for d in range(1, 8):
        spread(d, q).wait_send()
    own_slab.wait()
    own_rows.wait()


def gather_call(idx, tile, strip, slab):
    anywhere = pl.BlockSpec(memory_space=pl.ANY)
    vmem = pl.BlockSpec(memory_space=pltpu.VMEM)
    dma = pltpu.SemaphoreType.DMA
    return pl.pallas_call(
        gather_kernel,
        out_shape=(
            jax.ShapeDtypeStruct((STEPS, B, B), F32),
            jax.ShapeDtypeStruct((STEPS, B, B), F32),
            jax.ShapeDtypeStruct((STEPS, W, B), F32),
            jax.ShapeDtypeStruct((16, W, B), F32),
            jax.ShapeDtypeStruct((8, 1024, B), F32),
        ),
        in_specs=[pl.BlockSpec(memory_space=pltpu.SMEM), vmem, anywhere, anywhere],
        out_specs=(vmem, vmem, vmem, anywhere, anywhere),
        scratch_shapes=[
            pltpu.VMEM((16, 8, B), F32),
            pltpu.VMEM((STEPS, 8, B), F32),
            pltpu.VMEM((8, STEPS, 8, B), F32),
            pltpu.VMEM((STEPS, 16, 8, W), F32),
            pltpu.VMEM((16, B, B), F32),
            pltpu.VMEM((W, B), F32),
            dma((16,)), dma((16,)), dma((16,)), dma((16,)), dma((8,)), dma((8,)),
            dma((Ring.COUNT,)), dma((Ring.COUNT,)), dma, dma,
            dma((Ring.COUNT,)), dma((Ring.COUNT,)), dma((8,)), dma((8,)), dma((3,)),
        ],
        compiler_params=pltpu.CompilerParams(
            collective_id=0, has_side_effects=True, vmem_limit_bytes=56 * 2**20
        ),
        name="gather_factor",
    )(idx, tile, strip, slab)


def split(x):
    high = x.astype(BF16)
    return high, (x - high.astype(F32)).astype(BF16)


def dot3(a, b, dims):
    dot = functools.partial(lax.dot_general, dimension_numbers=dims, preferred_element_type=F32)
    return dot(a[0], b[0]) + (dot(a[0], b[1]) + dot(a[1], b[0]))


PAIR = 2 * B


def update_kernel(
    info, c0, c1, c2, c3, c4, c5, upper, inverse, lower, rows_ref, a_ref, o_ref,
    left_h, left_l, right_h, right_l,
):
    m = pl.program_id(0)
    k0, p, q = info[0], info[1], info[2]

    @pl.when(m == 0)
    def _():
        for b, c_ref in enumerate((c0, c1, c2, c3, c4, c5)):
            x = c_ref[0]
            if b:
                known = (left_h[:, : b * B], left_l[:, : b * B])
                strip = jnp.concatenate([lower[a, b * B : (b + 1) * B, :] for a in range(b)], 1)
                x = x - dot3(known, split(strip), NT)
            x = dot3(split(x), split(inverse[b]), NT)
            high, low = split(x)
            left_h[:, b * B : (b + 1) * B] = high
            left_l[:, b * B : (b + 1) * B] = low

    first = 2 * m * 8 + q
    second = first + 8
    last = k0 + STEPS - 1

    @pl.when(second > last)
    def _():
        for b in range(STEPS):
            x = jnp.concatenate(
                [rows_ref[0, b * B : (b + 1) * B, :], rows_ref[1, b * B : (b + 1) * B, :]], 1
            )
            if b:
                known = (right_h[: b * B, :], right_l[: b * B, :])
                strip = jnp.concatenate([lower[a, b * B : (b + 1) * B, :] for a in range(b)], 1)
                x = x - dot3(split(strip), known, NN)
            x = dot3(split(inverse[b]), split(x), NN)
            high, low = split(x)
            right_h[b * B : (b + 1) * B, :] = high
            right_l[b * B : (b + 1) * B, :] = low

    for part in range(4):

        @pl.when(m // 2 == part)
        def _():
            top = part * PAIR
            if part:
                o_ref[:top, :] = a_ref[:top, :]

            @pl.when(second > last)
            def _():
                count = 1024 - top
                update = dot3(
                    (left_h[top:, :], left_l[top:, :]), (right_h[...], right_l[...]), NN
                )
                row = (lax.broadcasted_iota(jnp.int32, (count, PAIR), 0) + top) // B * 16 + p
                col = lax.broadcasted_iota(jnp.int32, (count, PAIR), 1) // B * 8 + first
                keep = (row >= col) & (col > last)
                o_ref[top:, :] = a_ref[top:, :] - jnp.where(keep, update, 0.0)

            @pl.when(second <= last)
            def _():
                o_ref[top:, :] = a_ref[top:, :]

    for side in range(2):
        col = first + 8 * side
        lanes = slice(side * B, (side + 1) * B)
        for b in range(STEPS):

            @pl.when(col == k0 + b)
            def _():
                solved = left_h[:, b * B : (b + 1) * B].astype(F32) + left_l[
                    :, b * B : (b + 1) * B
                ].astype(F32)
                row = lax.broadcasted_iota(jnp.int32, (1024, B), 0) // B * 16 + p
                factor = jnp.concatenate([jnp.transpose(upper[b])] * 8, 0)
                o_ref[:, lanes] = jnp.where(
                    row > col, solved, jnp.where(row == col, factor, a_ref[:, lanes])
                )


def update_call(info, upper, inverse, lower, rout, cout, working):
    def column(b):
        return pl.BlockSpec((1, 1024, B), lambda m, info: (lax.rem(info[0] + b, 8), 0, 0))

    def fixed(shape):
        return pl.BlockSpec(shape, lambda m, info: (0,) * len(shape))

    return pl.pallas_call(
        update_kernel,
        out_shape=jax.ShapeDtypeStruct(working.shape, F32),
        grid_spec=pltpu.PrefetchScalarGridSpec(
            num_scalar_prefetch=1,
            grid=(8,),
            in_specs=[column(b) for b in range(STEPS)]
            + [
                fixed((STEPS, B, B)),
                fixed((STEPS, B, B)),
                fixed((STEPS, W, B)),
                pl.BlockSpec((2, W, B), lambda m, info: (m, 0, 0)),
                pl.BlockSpec((1024, PAIR), lambda m, info: (0, m)),
            ],
            out_specs=pl.BlockSpec((1024, PAIR), lambda m, info: (0, m)),
            scratch_shapes=[
                pltpu.VMEM((1024, W), BF16),
                pltpu.VMEM((1024, W), BF16),
                pltpu.VMEM((W, PAIR), BF16),
                pltpu.VMEM((W, PAIR), BF16),
            ],
        ),
        compiler_params=pltpu.CompilerParams(vmem_limit_bytes=56 * 2**20),
        name="update",
    )(info, *([cout] * STEPS), upper, inverse, lower, rout, working)


def local(working, step):
    p = lax.axis_index("row").astype(jnp.int32)
    q = lax.axis_index("col").astype(jnp.int32)
    k0 = step[0]
    turns = jnp.arange(STEPS, dtype=jnp.int32)
    idx = jnp.concatenate([(k0 + turns) % 16, (k0 + turns) % 8])
    t = jnp.minimum((k0 + (p - k0) % 16) // 16, 7)
    c = jnp.minimum((k0 + (q - k0) % 8) // 8, 15)
    strip = lax.dynamic_slice(working, (t * B, 0), (B, 2048))
    slab = lax.dynamic_slice(working, (0, c * B), (1024, B))
    tile = lax.dynamic_slice(working, (t * B, c * B), (B, B))
    upper, inverse, lower, rout, cout = gather_call(idx, tile, strip, slab)
    info = jnp.stack([k0, p, q])
    return update_call(info, upper, inverse, lower, rout, cout, working)


def solution(mesh):
    placed = (P("row", "col"), P())
    return jax.shard_map(
        local, mesh=mesh, in_specs=placed, out_specs=P("row", "col"), check_vma=False
    )
```

```python
import functools

import jax
import jax.numpy as jnp
from jax import lax
from jax.experimental import pallas as pl
from jax.experimental.pallas import tpu as pltpu
from jax.sharding import PartitionSpec as P

B = 128
STEPS = 6
W = B * STEPS
F32 = jnp.float32
BF16 = jnp.bfloat16
MESH = pl.DeviceIdType.MESH
HIGHEST = lax.Precision.HIGHEST
NT = (((1,), (1,)), ((), ()))
NN = (((1,), (0,)), ((), ()))


def factor_tile(tile):
    chunk = 8
    rest = tile
    other = (
        lax.broadcasted_iota(jnp.int32, (B, B), 0) == lax.broadcasted_iota(jnp.int32, (B, B), 1)
    ).astype(F32)
    uppers, inverses = [], []
    for first in range(0, B, chunk):
        rows = B - first
        row = lax.broadcasted_iota(jnp.int32, (rows, B), 0)
        coefs = [
            jnp.broadcast_to(rest[:, first + i : first + i + 1], (rows, B)) for i in range(chunk)
        ]
        scales = []
        for j in range(chunk):
            scale = lax.rsqrt(coefs[j][j : j + 1, :])
            scales.append(scale)
            factor = jnp.where(row > j, coefs[j] * (scale * scale), 0.0)
            rest = rest - factor * rest[j : j + 1, :]
            other = other - factor * other[j : j + 1, :]
            for i in range(j + 1, chunk):
                coefs[i] = coefs[i] - factor * coefs[i][j : j + 1, :]
        scale = jnp.concatenate(scales, 0)
        sub = lax.broadcasted_iota(jnp.int32, (chunk, B), 0)
        lane = lax.broadcasted_iota(jnp.int32, (chunk, B), 1)
        uppers.append(jnp.where(lane >= first + sub, rest[:chunk] * scale, 0.0))
        inverses.append(other[:chunk] * scale)
        rest, other = rest[chunk:], other[chunk:]
    return jnp.concatenate(uppers, 0), jnp.concatenate(inverses, 0)


class Ring:
    MESSAGES = (
        (
            ((0, 0), None, (1, 0)),
            ((0, 0), None, (-1, 0)),
            ((0, 0), None, (0, 1)),
            ((0, 0), None, (0, -1)),
        ),
        (
            ((-1, 0), 0, (1, 0)),
            ((1, 0), 1, (-1, 0)),
            ((0, -1), 0, (0, 1)),
            ((0, 1), 1, (0, -1)),
            ((-1, 0), None, (0, 1)),
            ((-1, 0), None, (0, -1)),
            ((1, 0), None, (0, 1)),
            ((1, 0), None, (0, -1)),
        ),
        (
            ((2, 0), None, (0, 1)),
            ((2, 0), None, (0, -1)),
            ((-1, -1), 0, (0, 1)),
            ((1, -1), 0, (0, 1)),
            ((-1, 1), 1, (0, -1)),
            ((1, 1), 1, (0, -1)),
        ),
        (
            ((2, -1), 0, (0, 1)),
            ((2, 1), 1, (0, -1)),
        ),
    )
    COUNT = 20

    def __init__(self, row, col, view, own, send_sem, recv_sem):
        core = lax.rem(col, 2)
        x, z = row // 4, lax.rem(row, 4)
        self.u = z + core * (x - z)
        self.v = x + core * (z - x)
        self.su, self.sv = 1 + 3 * core, 4 - 3 * core
        self.col, self.view, self.own = col, view, own
        self.send_sem, self.recv_sem = send_sem, recv_sem

    def index(self, du, dv):
        return self.su * lax.rem(self.u + du + 4, 4) + self.sv * lax.rem(self.v + dv + 4, 4)

    def copy(self, number, message, receiving):
        (du, dv), part, (au, av) = message
        if receiving:
            du, dv = du - au, dv - av
        block = self.index(du, dv)
        dst = self.view(block, part)
        src = self.own if (du, dv) == (0, 0) and not receiving and self.own is not None else dst
        return pltpu.make_async_remote_copy(
            src_ref=src,
            dst_ref=dst,
            send_sem=self.send_sem.at[number],
            recv_sem=self.recv_sem.at[number],
            device_id=(self.index(au, av), self.col),
            device_id_type=MESH,
        )

    def numbered(self, tick):
        base = sum(len(m) for m in self.MESSAGES[:tick])
        return [(base + i, m) for i, m in enumerate(self.MESSAGES[tick])]

    def tick(self, tick):
        if tick > 0:
            for number, message in self.numbered(tick - 1):
                self.copy(number, message, True).wait_recv()
        if tick < len(self.MESSAGES):
            for number, message in self.numbered(tick):
                self.copy(number, message, False).start()

    def finish(self):
        for tick in range(len(self.MESSAGES)):
            for number, message in self.numbered(tick):
                self.copy(number, message, False).wait_send()


def gather_kernel(
    step_ref, working,
    upper_o, inverse_o, rout, cout,
    staged, tile, strip, slab, dbuf, dcol, dcg, whole, rbuf, bst,
    d1s, d1r, a1s, a1r, d2s, d2r, d3s, d3r, sibs, sibr, rs, rr, cs, cr, local,
):
    p, q = lax.axis_index("row"), lax.axis_index("col")
    core, y = lax.rem(q, 2), q // 2
    sibling = q + 1 - 2 * core
    k0 = step_ref[0]

    stages = [
        pltpu.make_async_copy(
            working.at[:, :, pl.ds(j * B, B)], staged.at[j], local.at[2 + j]
        )
        for j in range(16)
    ]
    for stage in stages:
        stage.start()
    barrier = pltpu.get_barrier_semaphore()
    for d in range(1, 16):
        pl.semaphore_signal(barrier, inc=1, device_id=(lax.rem(p + d, 16), q), device_id_type=MESH)
    for d in range(1, 8):
        pl.semaphore_signal(barrier, inc=1, device_id=(p, lax.rem(q + d, 8)), device_id_type=MESH)
    pl.semaphore_wait(barrier, 22)
    for stage in stages:
        stage.wait()

    t = jnp.minimum(lax.div(k0 + lax.rem(p - k0 + 128, 16), 16), 7)
    c = jnp.minimum(lax.div(k0 + lax.rem(q - k0 + 128, 8), 8), 15)
    tile[...] = staged[c, t]

    def remote(src, dst, send, recv, device):
        return pltpu.make_async_remote_copy(
            src_ref=src, dst_ref=dst, send_sem=send, recv_sem=recv,
            device_id=device, device_id_type=MESH,
        )

    def diag(d, slot):
        to = lax.rem(p + d, 16)
        rows = pl.ds(pl.multiple_of(8 * to, 8), 8)
        return remote(tile.at[rows, :], dbuf.at[slot], d1s.at[d], d1r.at[d], (to, q))

    def piece(d, slot):
        to = lax.rem(p + d, 16)
        return remote(strip.at[to], rbuf.at[slot], a1s.at[d], a1r.at[d], (to, q))

    def spread(d, slot):
        to = lax.rem(q + d, 8)
        return remote(dcol, dcg.at[slot], d2s.at[d], d2r.at[d], (p, to))

    for d in range(1, 16):
        diag(d, p).start()
    for j in range(16):
        strip[j] = staged[j, t]
    for d in range(1, 16):
        piece(d, p).start()
    rbuf[p] = strip[p]
    slab[...] = staged[c].reshape(1024, B)
    own_slab = pltpu.make_async_copy(slab, cout.at[q], local.at[1])
    own_slab.start()
    dbuf[p] = tile[pl.ds(pl.multiple_of(8 * p, 8), 8), :]
    for d in range(1, 16):
        diag(d, lax.rem(p + 16 - d, 16)).wait_recv()
    for s in range(STEPS):
        block = dbuf[lax.rem(k0 + s, 16)]
        dcol[s] = block
        dcg[q, s] = block
    for d in range(1, 8):
        spread(d, q).start()

    def slot(dy):
        return lax.rem(y + dy + 4, 4) * 2 + core

    def part_of(block, part):
        return cout.at[block] if part is None else cout.at[block, pl.ds(512 * part, 512), :]

    def along(n, dy, part, ay, receiving):
        block = slot(dy - ay if receiving else dy)
        dst = part_of(block, part)
        src = slab if dy == 0 and not receiving else dst
        return remote(src, dst, cs.at[n], cr.at[n], (p, slot(ay)))

    def across(n, dy, receiving):
        block = slot(dy) + 1 - 2 * core if receiving else slot(dy)
        src = slab if dy == 0 and not receiving else cout.at[block]
        return remote(src, cout.at[block], cs.at[n], cr.at[n], (p, sibling))

    along_messages = ((0, 0, None, 1), (1, 0, None, -1), (3, -1, 0, 1), (4, 1, 1, -1))
    across_messages = ((2, 0), (5, -1), (6, 1), (7, 2))

    def columns_tick(tick):
        if tick == 0:
            along(*along_messages[0], False).start()
            along(*along_messages[1], False).start()
            across(*across_messages[0], False).start()
        elif tick == 1:
            along(*along_messages[0], True).wait_recv()
            along(*along_messages[1], True).wait_recv()
            along(*along_messages[2], False).start()
            along(*along_messages[3], False).start()
            across(*across_messages[1], False).start()
            across(*across_messages[2], False).start()
        elif tick == 2:
            along(*along_messages[2], True).wait_recv()
            along(*along_messages[3], True).wait_recv()
            across(*across_messages[3], False).start()
        else:
            for message in across_messages:
                across(*message, True).wait_recv()
            for message in along_messages:
                along(*message, False).wait_send()
            for message in across_messages:
                across(*message, False).wait_send()

    for d in range(1, 8):
        spread(d, lax.rem(q + 8 - d, 8)).wait_recv()
    half = pl.ds(3 * core, 3)
    for b in range(STEPS):
        whole[half, p, :, b * B : (b + 1) * B] = dcg[lax.rem(k0 + b, 8), half]

    def diag_view(block, part):
        if part is None:
            return whole.at[half, block]
        return whole.at[half, block, :, pl.ds(384 * part, 384)]

    def row_view(block, part):
        return rout.at[block] if part is None else rout.at[block, pl.ds(384 * part, 384), :]

    diag_ring = Ring(p, q, diag_view, None, d3s, d3r)
    row_ring = Ring(p, q, row_view, bst, rs, rr)
    diag_ring.tick(0)
    columns_tick(0)

    for d in range(1, 16):
        piece(d, lax.rem(p + 16 - d, 16)).wait_recv()
    for s in range(STEPS):
        bst[s * B : (s + 1) * B, :] = rbuf[lax.rem(k0 + s, 16)]
    own_rows = pltpu.make_async_copy(bst, rout.at[p], local.at[0])
    own_rows.start()
    row_ring.tick(0)
    diag_ring.tick(1)
    diag_ring.tick(2)
    diag_ring.tick(3)
    columns_tick(1)
    diag_ring.tick(4)
    other = pl.ds(3 - 3 * core, 3)
    to_sibling = remote(whole.at[half], whole.at[half], sibs, sibr, (p, sibling))
    from_sibling = remote(whole.at[other], whole.at[other], sibs, sibr, (p, sibling))
    to_sibling.start()
    row_ring.tick(1)
    from_sibling.wait_recv()
    to_sibling.wait_send()
    diag_ring.finish()

    def step(k, carry):
        here = pl.ds(pl.multiple_of(k * B, B), B)
        upper, inverse = factor_tile(whole[k, :, :, here].reshape(B, B))
        upper_o[k] = upper
        dot = functools.partial(
            lax.dot_general, precision=HIGHEST, preferred_element_type=F32
        )
        for i in range(STEPS):

            @pl.when(k == i)
            def _():
                at = slice(i * B, (i + 1) * B)
                inverse_o[at, at] = inverse
                if i:
                    known = whole[i, :, :, : i * B].reshape(B, i * B)
                    inverse_o[at, : i * B] = dot(inverse, known, NN)
                if i < STEPS - 1:
                    left = STEPS - 1 - i
                    inverse_o[at, (i + 1) * B :] = jnp.zeros((B, left * B), F32)
                    below = whole[i + 1 :, :, :, at].reshape(left * B, B)
                    solved = dot(below, inverse, NT)
                    update = dot(solved, solved, NT)
                    whole[i + 1 :, :, :, (i + 1) * B :] = whole[
                        i + 1 :, :, :, (i + 1) * B :
                    ] - update.reshape(left, 16, 8, left * B)
                    update = dot(solved, inverse_o[at, : (i + 1) * B], NN)
                    update = update.reshape(left, 16, 8, (i + 1) * B)
                    if i:
                        whole[i + 1 :, :, :, : i * B] = (
                            whole[i + 1 :, :, :, : i * B] - update[:, :, :, : i * B]
                        )
                    whole[i + 1 :, :, :, at] = -update[:, :, :, i * B :]
                if i == 0:
                    columns_tick(2)
                if i == 1:
                    row_ring.tick(2)
                if i == 3:
                    row_ring.tick(3)
                if i == 5:
                    row_ring.tick(4)

        return carry

    lax.fori_loop(0, STEPS, step, 0)
    columns_tick(3)
    row_ring.finish()
    for d in range(1, 16):
        diag(d, p).wait_send()
        piece(d, p).wait_send()
    for d in range(1, 8):
        spread(d, q).wait_send()
    own_slab.wait()
    own_rows.wait()


def gather_call(step, working):
    anywhere = pl.BlockSpec(memory_space=pl.ANY)
    vmem = pl.BlockSpec(memory_space=pltpu.VMEM)
    dma = pltpu.SemaphoreType.DMA
    return pl.pallas_call(
        gather_kernel,
        out_shape=(
            jax.ShapeDtypeStruct((STEPS, B, B), F32),
            jax.ShapeDtypeStruct((W, W), F32),
            jax.ShapeDtypeStruct((16, W, B), F32),
            jax.ShapeDtypeStruct((8, 1024, B), F32),
        ),
        in_specs=[pl.BlockSpec(memory_space=pltpu.SMEM), anywhere],
        out_specs=(vmem, vmem, anywhere, anywhere),
        scratch_shapes=[
            pltpu.VMEM((16, 8, B, B), F32),
            pltpu.VMEM((B, B), F32),
            pltpu.VMEM((16, B, B), F32),
            pltpu.VMEM((1024, B), F32),
            pltpu.VMEM((16, 8, B), F32),
            pltpu.VMEM((STEPS, 8, B), F32),
            pltpu.VMEM((8, STEPS, 8, B), F32),
            pltpu.VMEM((STEPS, 16, 8, W), F32),
            pltpu.VMEM((16, B, B), F32),
            pltpu.VMEM((W, B), F32),
            dma((16,)), dma((16,)), dma((16,)), dma((16,)), dma((8,)), dma((8,)),
            dma((Ring.COUNT,)), dma((Ring.COUNT,)), dma, dma,
            dma((Ring.COUNT,)), dma((Ring.COUNT,)), dma((8,)), dma((8,)), dma((18,)),
        ],
        compiler_params=pltpu.CompilerParams(
            collective_id=0, has_side_effects=True, vmem_limit_bytes=56 * 2**20
        ),
        name="gather_factor",
    )(step, working.reshape(8, B, 2048))


def split(x):
    high = x.astype(BF16)
    return high, (x - high.astype(F32)).astype(BF16)


def dot3(a, b, dims):
    dot = functools.partial(lax.dot_general, dimension_numbers=dims, preferred_element_type=F32)
    return dot(a[0], b[0]) + (dot(a[0], b[1]) + dot(a[1], b[0]))


PAIR = 2 * B


def update_kernel(
    info, c0, c1, c2, c3, c4, c5, upper, inverse, rows_ref, a_ref, o_ref,
    inverse_h, inverse_l, left_h, left_l, right_h, right_l,
):
    m = pl.program_id(0)
    k0, p, q = info[0], lax.axis_index("row"), lax.axis_index("col")

    @pl.when(m == 0)
    def _():
        inverse_h[...], inverse_l[...] = split(inverse[...])
        parts = [split(c_ref[0]) for c_ref in (c0, c1, c2, c3, c4, c5)]
        for b in range(0, STEPS, 2):
            end = (b + 2) * B
            at = slice(b * B, end)
            known = [jnp.concatenate([part[i] for part in parts[: b + 2]], 1) for i in range(2)]
            x = dot3(known, (inverse_h[at, :end], inverse_l[at, :end]), NT)
            left_h[:, at], left_l[:, at] = split(x)

    first = 2 * m * 8 + q
    second = first + 8
    last = k0 + STEPS - 1

    @pl.when(second > last)
    def _():
        x = split(jnp.concatenate([rows_ref[0], rows_ref[1]], 1))
        for b in range(0, STEPS, 2):
            end = (b + 2) * B
            at = slice(b * B, end)
            y = dot3((inverse_h[at, :end], inverse_l[at, :end]), (x[0][:end], x[1][:end]), NN)
            right_h[at, :], right_l[at, :] = split(y)

    for part in range(4):

        @pl.when(m // 2 == part)
        def _():
            top = part * PAIR
            if part:
                o_ref[:top, :] = a_ref[:top, :]

            @pl.when(second > last)
            def _():
                count = 1024 - top
                update = dot3(
                    (left_h[top:, :], left_l[top:, :]), (right_h[...], right_l[...]), NN
                )
                row = (lax.broadcasted_iota(jnp.int32, (count, PAIR), 0) + top) // B * 16 + p
                col = lax.broadcasted_iota(jnp.int32, (count, PAIR), 1) // B * 8 + first
                keep = (row >= col) & (col > last)
                o_ref[top:, :] = a_ref[top:, :] - jnp.where(keep, update, 0.0)

            @pl.when(second <= last)
            def _():
                o_ref[top:, :] = a_ref[top:, :]

    for side in range(2):
        col = first + 8 * side
        lanes = slice(side * B, (side + 1) * B)
        for b in range(STEPS):

            @pl.when(col == k0 + b)
            def _():
                solved = left_h[:, b * B : (b + 1) * B].astype(F32) + left_l[
                    :, b * B : (b + 1) * B
                ].astype(F32)
                row = lax.broadcasted_iota(jnp.int32, (1024, B), 0) // B * 16 + p
                factor = jnp.concatenate([jnp.transpose(upper[b])] * 8, 0)
                o_ref[:, lanes] = jnp.where(
                    row > col, solved, jnp.where(row == col, factor, a_ref[:, lanes])
                )


def update_call(step, upper, inverse, rout, cout, working):
    def column(b):
        return pl.BlockSpec((1, 1024, B), lambda m, info: (lax.rem(info[0] + b, 8), 0, 0))

    def fixed(shape):
        return pl.BlockSpec(shape, lambda m, info: (0,) * len(shape))

    return pl.pallas_call(
        update_kernel,
        out_shape=jax.ShapeDtypeStruct(working.shape, F32),
        grid_spec=pltpu.PrefetchScalarGridSpec(
            num_scalar_prefetch=1,
            grid=(8,),
            in_specs=[column(b) for b in range(STEPS)]
            + [
                fixed((STEPS, B, B)),
                fixed((W, W)),
                pl.BlockSpec((2, W, B), lambda m, info: (m, 0, 0)),
                pl.BlockSpec((1024, PAIR), lambda m, info: (0, m)),
            ],
            out_specs=pl.BlockSpec((1024, PAIR), lambda m, info: (0, m)),
            scratch_shapes=[
                pltpu.VMEM((W, W), BF16),
                pltpu.VMEM((W, W), BF16),
                pltpu.VMEM((1024, W), BF16),
                pltpu.VMEM((1024, W), BF16),
                pltpu.VMEM((W, PAIR), BF16),
                pltpu.VMEM((W, PAIR), BF16),
            ],
        ),
        compiler_params=pltpu.CompilerParams(vmem_limit_bytes=56 * 2**20),
        name="update",
    )(step, *([cout] * STEPS), upper, inverse, rout, working)


def local(working, step):
    upper, inverse, rout, cout = gather_call(step, working)
    return update_call(step, upper, inverse, rout, cout, working)


def solution(mesh):
    placed = (P("row", "col"), P())
    return jax.shard_map(
        local, mesh=mesh, in_specs=placed, out_specs=P("row", "col"), check_vma=False
    )
```

```python
import functools

import jax
import jax.numpy as jnp
from jax import lax
from jax.experimental import pallas as pl
from jax.experimental.pallas import tpu as pltpu
from jax.sharding import PartitionSpec as P

B = 128
STEPS = 6
W = B * STEPS
LOWER = [(a, b) for a in range(STEPS) for b in range(a + 1)]
F32 = jnp.float32
BF16 = jnp.bfloat16
MESH = pl.DeviceIdType.MESH
HIGHEST = lax.Precision.HIGHEST
NT = (((1,), (1,)), ((), ()))
NN = (((1,), (0,)), ((), ()))


def factor_tile(tile, hook):
    sub = lax.broadcasted_iota(jnp.int32, (8, B), 0)
    lane = lax.broadcasted_iota(jnp.int32, (8, B), 1)
    lanes = lax.broadcasted_iota(jnp.int32, (B, B), 1)

    def spread(x, first):
        return [jnp.broadcast_to(x[:, first + i : first + i + 1], x.shape) for i in range(8)]

    head, rest = tile[:8], tile[8:]
    held = spread(head, 0)
    uppers, inverses = [], []
    for first in range(0, B, 8):
        if first == B // 2:
            hook()
        more = first + 8 < B
        if more:
            coefs = spread(rest, first)
            head_next = spread(head, first + 8)
            rest_next = spread(rest[:8], first + 8)
            at = lanes[: B - first - 8]
            rest = jnp.where((at >= first) & (at < first + 8), 0.0, rest)
        inside = (lane >= first) & (lane < first + 8)
        head = jnp.where(inside, jnp.where(lane - first == sub, 1.0, 0.0), head)
        scales = []
        for j in range(8):
            pivot = held[j][j : j + 1]
            inverse = 1.0 / pivot
            scales.append(lax.rsqrt(pivot))
            factor = jnp.where(sub > j, held[j] * inverse, 0.0)
            row = head[j : j + 1]
            cross = [held[i][j : j + 1] for i in range(8)]
            for i in range(j + 1, 8):
                held[i] = held[i] - factor * cross[i]
            if more:
                further = [head_next[i][j : j + 1] for i in range(8)]
            head = head - factor * row
            if more:
                below = coefs[j] * inverse
                for i in range(j + 1, 8):
                    coefs[i] = coefs[i] - below * cross[i]
                rest = rest - below * row
                for i in range(8):
                    head_next[i] = head_next[i] - factor * further[i]
                    rest_next[i] = rest_next[i] - below[:8] * further[i]
        scale = jnp.concatenate(scales, 0)
        done = head * scale
        upper = jnp.where(lane >= first + 8, done, 0.0)
        for i in range(8):
            upper = jnp.where((lane == first + i) & (sub <= i), held[i] * scale, upper)
        uppers.append(upper)
        inverses.append(jnp.where(lane < first + 8, done, 0.0))
        if more:
            held = rest_next
            head, rest = rest[:8], rest[8:]
    return jnp.concatenate(uppers, 0), jnp.concatenate(inverses, 0)


class Ring:
    MESSAGES = (
        (
            ((0, 0), None, (1, 0)),
            ((0, 0), None, (-1, 0)),
            ((0, 0), None, (0, 1)),
            ((0, 0), None, (0, -1)),
        ),
        (
            ((-1, 0), 0, (1, 0)),
            ((1, 0), 1, (-1, 0)),
            ((0, -1), 0, (0, 1)),
            ((0, 1), 1, (0, -1)),
            ((-1, 0), None, (0, 1)),
            ((-1, 0), None, (0, -1)),
            ((1, 0), None, (0, 1)),
            ((1, 0), None, (0, -1)),
        ),
        (
            ((2, 0), None, (0, 1)),
            ((2, 0), None, (0, -1)),
            ((-1, -1), 0, (0, 1)),
            ((1, -1), 0, (0, 1)),
            ((-1, 1), 1, (0, -1)),
            ((1, 1), 1, (0, -1)),
        ),
        (
            ((2, -1), 0, (0, 1)),
            ((2, 1), 1, (0, -1)),
        ),
    )
    COUNT = 20

    def __init__(self, row, col, view, own, send_sem, recv_sem):
        core = lax.rem(col, 2)
        x, z = row // 4, lax.rem(row, 4)
        self.u = z + core * (x - z)
        self.v = x + core * (z - x)
        self.su, self.sv = 1 + 3 * core, 4 - 3 * core
        self.col, self.view, self.own = col, view, own
        self.send_sem, self.recv_sem = send_sem, recv_sem

    def index(self, du, dv):
        return self.su * lax.rem(self.u + du + 4, 4) + self.sv * lax.rem(self.v + dv + 4, 4)

    def copy(self, number, message, receiving):
        (du, dv), part, (au, av) = message
        if receiving:
            du, dv = du - au, dv - av
        block = self.index(du, dv)
        dst = self.view(block, part)
        src = self.own if (du, dv) == (0, 0) and not receiving and self.own is not None else dst
        return pltpu.make_async_remote_copy(
            src_ref=src,
            dst_ref=dst,
            send_sem=self.send_sem.at[number],
            recv_sem=self.recv_sem.at[number],
            device_id=(self.index(au, av), self.col),
            device_id_type=MESH,
        )

    def numbered(self, tick):
        base = sum(len(m) for m in self.MESSAGES[:tick])
        return [(base + i, m) for i, m in enumerate(self.MESSAGES[tick])]

    def tick(self, tick):
        if tick > 0:
            for number, message in self.numbered(tick - 1):
                self.copy(number, message, True).wait_recv()
        if tick < len(self.MESSAGES):
            for number, message in self.numbered(tick):
                self.copy(number, message, False).start()

    def finish(self):
        for tick in range(len(self.MESSAGES)):
            for number, message in self.numbered(tick):
                self.copy(number, message, False).wait_send()


def gather_kernel(
    step_ref, working,
    upper_o, inverse_o, rout, cout,
    staged, tile, strip, slab, dbuf, dcol, dcg, dall, packed, whole, rbuf, bst,
    d1s, d1r, a1s, a1r, d2s, d2r, d3s, d3r, sibs, sibr, rs, rr, rs2, rr2, cs, cr, local,
):
    p, q = lax.axis_index("row"), lax.axis_index("col")
    core, y = lax.rem(q, 2), q // 2
    sibling = q + 1 - 2 * core
    k0 = step_ref[0]

    stages = [
        pltpu.make_async_copy(
            working.at[:, :, pl.ds(j * B, B)], staged.at[j], local.at[2 + j]
        )
        for j in range(16)
    ]
    for stage in stages:
        stage.start()
    barrier = pltpu.get_barrier_semaphore()
    for d in range(1, 16):
        pl.semaphore_signal(barrier, inc=1, device_id=(lax.rem(p + d, 16), q), device_id_type=MESH)
    for d in range(1, 8):
        pl.semaphore_signal(barrier, inc=1, device_id=(p, lax.rem(q + d, 8)), device_id_type=MESH)
    pl.semaphore_wait(barrier, 22)
    for stage in stages:
        stage.wait()

    t = jnp.minimum(lax.div(k0 + lax.rem(p - k0 + 128, 16), 16), 7)
    c = jnp.minimum(lax.div(k0 + lax.rem(q - k0 + 128, 8), 8), 15)
    tile[...] = staged[c, t]

    def remote(src, dst, send, recv, device):
        return pltpu.make_async_remote_copy(
            src_ref=src, dst_ref=dst, send_sem=send, recv_sem=recv,
            device_id=device, device_id_type=MESH,
        )

    def diag(d, slot):
        to = lax.rem(p + d, 16)
        rows = pl.ds(pl.multiple_of(8 * to, 8), 8)
        return remote(tile.at[rows, :], dbuf.at[slot], d1s.at[d], d1r.at[d], (to, q))

    def piece(d, slot):
        to = lax.rem(p + d, 16)
        return remote(strip.at[to], rbuf.at[slot], a1s.at[d], a1r.at[d], (to, q))

    def spread(d, slot):
        to = lax.rem(q + d, 8)
        return remote(dcol, dcg.at[slot], d2s.at[d], d2r.at[d], (p, to))

    for d in range(1, 16):
        diag(d, p).start()
    for j in range(16):
        strip[j] = staged[j, t]
    for d in range(1, 16):
        piece(d, p).start()
    rbuf[p] = strip[p]
    slab[...] = staged[c].reshape(1024, B)
    own_slab = pltpu.make_async_copy(slab, cout.at[q], local.at[1])
    own_slab.start()
    dbuf[p] = tile[pl.ds(pl.multiple_of(8 * p, 8), 8), :]
    for d in range(1, 16):
        diag(d, lax.rem(p + 16 - d, 16)).wait_recv()
    for s in range(STEPS):
        block = dbuf[lax.rem(k0 + s, 16)]
        dcol[s] = block
        dcg[q, s] = block
    for d in range(1, 8):
        spread(d, q).start()

    def slot(dy):
        return lax.rem(y + dy + 4, 4) * 2 + core

    def part_of(block, part):
        return cout.at[block] if part is None else cout.at[block, pl.ds(512 * part, 512), :]

    def along(n, dy, part, ay, receiving):
        block = slot(dy - ay if receiving else dy)
        dst = part_of(block, part)
        src = slab if dy == 0 and not receiving else dst
        return remote(src, dst, cs.at[n], cr.at[n], (p, slot(ay)))

    def across(n, dy, receiving):
        block = slot(dy) + 1 - 2 * core if receiving else slot(dy)
        src = slab if dy == 0 and not receiving else cout.at[block]
        return remote(src, cout.at[block], cs.at[n], cr.at[n], (p, sibling))

    along_messages = ((0, 0, None, 1), (1, 0, None, -1), (3, -1, 0, 1), (4, 1, 1, -1))
    across_messages = ((2, 0), (5, -1), (6, 1), (7, 2))

    def columns_tick(tick):
        if tick == 0:
            along(*along_messages[0], False).start()
            along(*along_messages[1], False).start()
        elif tick == 1:
            across(*across_messages[0], False).start()
            along(*along_messages[0], True).wait_recv()
            along(*along_messages[1], True).wait_recv()
            along(*along_messages[2], False).start()
            along(*along_messages[3], False).start()
            across(*across_messages[1], False).start()
            across(*across_messages[2], False).start()
        elif tick == 2:
            along(*along_messages[2], True).wait_recv()
            along(*along_messages[3], True).wait_recv()
            across(*across_messages[3], False).start()
        else:
            for message in across_messages:
                across(*message, True).wait_recv()
            for message in along_messages:
                along(*message, False).wait_send()
            for message in across_messages:
                across(*message, False).wait_send()

    for d in range(1, 8):
        spread(d, lax.rem(q + 8 - d, 8)).wait_recv()
    for n, (a, b) in enumerate(LOWER):
        dall[n] = dcg[lax.rem(k0 + b, 8), a]
    dall[len(LOWER)] = jnp.zeros((8, B), F32)
    half = pl.ds(11 * core, 11)
    packed[p, half] = dall[half]

    def block(d, slot):
        mine = packed.at[slot, half]
        return remote(mine, mine, d3s.at[d], d3r.at[d], (lax.rem(p + d, 16), q))

    def row_view(stream):
        def view(block, part):
            if part is None:
                return rout.at[block, pl.ds(384 * stream, 384), :]
            return rout.at[block, pl.ds(384 * stream + 192 * part, 192), :]

        return view

    streams = [
        Ring(p, q, row_view(0), bst.at[:384], rs, rr),
        Ring(p, q, row_view(1), bst.at[384:], rs2, rr2),
    ]
    for d in range(1, 16):
        block(d, p).start()
    columns_tick(0)

    for d in range(1, 16):
        piece(d, lax.rem(p + 16 - d, 16)).wait_recv()
    for s in range(STEPS):
        bst[s * B : (s + 1) * B, :] = rbuf[lax.rem(k0 + s, 16)]
    own_rows = pltpu.make_async_copy(bst, rout.at[p], local.at[0])
    own_rows.start()
    streams[0].tick(0)
    streams[1].tick(0)
    for d in range(1, 16):
        block(d, lax.rem(p + 16 - d, 16)).wait_recv()
    other = pl.ds(11 - 11 * core, 11)
    to_sibling = remote(packed.at[:, half], packed.at[:, half], sibs, sibr, (p, sibling))
    from_sibling = remote(packed.at[:, other], packed.at[:, other], sibs, sibr, (p, sibling))
    to_sibling.start()
    streams[0].tick(1)
    from_sibling.wait_recv()
    for n, (a, b) in enumerate(LOWER):
        whole[a, :, :, b * B : (b + 1) * B] = packed[:, n]

    def run(ring_tick, first, column_tick, second):
        ring_tick(first)
        column_tick(second)

    ticks = {
        (0, 1): lambda: run(streams[1].tick, 1, columns_tick, 1),
        (1, 1): lambda: run(streams[0].tick, 2, columns_tick, 2),
        (2, 1): lambda: streams[1].tick(2),
        (3, 1): lambda: streams[0].tick(3),
        (4, 1): lambda: streams[1].tick(3),
    }

    def tick(k, place):
        for (step, where), call in ticks.items():
            if where == place:
                pl.when(k == step)(call)

    def step(k, carry):
        here = pl.ds(pl.multiple_of(k * B, B), B)
        upper, inverse = factor_tile(
            whole[k, :, :, here].reshape(B, B), lambda: tick(k, 0)
        )
        upper_o[k] = upper
        dot = functools.partial(
            lax.dot_general, precision=HIGHEST, preferred_element_type=F32
        )
        for i in range(STEPS):

            @pl.when(k == i)
            def _():
                at = slice(i * B, (i + 1) * B)
                inverse_o[at, at] = inverse
                if i:
                    known = whole[i, :, :, : i * B].reshape(B, i * B)
                    inverse_o[at, : i * B] = dot(inverse, known, NN)
                if i < STEPS - 1:
                    left = STEPS - 1 - i
                    inverse_o[at, (i + 1) * B :] = jnp.zeros((B, left * B), F32)
                    below = whole[i + 1 :, :, :, at].reshape(left * B, B)
                    solved = dot(below, inverse, NT)
                    update = dot(solved, solved, NT)
                    whole[i + 1 :, :, :, (i + 1) * B :] = whole[
                        i + 1 :, :, :, (i + 1) * B :
                    ] - update.reshape(left, 16, 8, left * B)
                    update = dot(solved, inverse_o[at, : (i + 1) * B], NN)
                    update = update.reshape(left, 16, 8, (i + 1) * B)
                    if i:
                        whole[i + 1 :, :, :, : i * B] = (
                            whole[i + 1 :, :, :, : i * B] - update[:, :, :, : i * B]
                        )
                    whole[i + 1 :, :, :, at] = -update[:, :, :, i * B :]

        tick(k, 1)
        return carry

    lax.fori_loop(0, STEPS, step, 0)
    columns_tick(3)
    for stream in streams:
        stream.tick(4)
        stream.finish()
    to_sibling.wait_send()
    for d in range(1, 16):
        block(d, p).wait_send()
    for d in range(1, 16):
        diag(d, p).wait_send()
        piece(d, p).wait_send()
    for d in range(1, 8):
        spread(d, q).wait_send()
    own_slab.wait()
    own_rows.wait()


def gather_call(step, working):
    anywhere = pl.BlockSpec(memory_space=pl.ANY)
    vmem = pl.BlockSpec(memory_space=pltpu.VMEM)
    dma = pltpu.SemaphoreType.DMA
    return pl.pallas_call(
        gather_kernel,
        out_shape=(
            jax.ShapeDtypeStruct((STEPS, B, B), F32),
            jax.ShapeDtypeStruct((W, W), F32),
            jax.ShapeDtypeStruct((16, W, B), F32),
            jax.ShapeDtypeStruct((8, 1024, B), F32),
        ),
        in_specs=[pl.BlockSpec(memory_space=pltpu.SMEM), anywhere],
        out_specs=(vmem, vmem, anywhere, anywhere),
        scratch_shapes=[
            pltpu.VMEM((16, 8, B, B), F32),
            pltpu.VMEM((B, B), F32),
            pltpu.VMEM((16, B, B), F32),
            pltpu.VMEM((1024, B), F32),
            pltpu.VMEM((16, 8, B), F32),
            pltpu.VMEM((STEPS, 8, B), F32),
            pltpu.VMEM((8, STEPS, 8, B), F32),
            pltpu.VMEM((22, 8, B), F32),
            pltpu.VMEM((16, 22, 8, B), F32),
            pltpu.VMEM((STEPS, 16, 8, W), F32),
            pltpu.VMEM((16, B, B), F32),
            pltpu.VMEM((W, B), F32),
            dma((16,)), dma((16,)), dma((16,)), dma((16,)), dma((8,)), dma((8,)),
            dma((Ring.COUNT,)), dma((Ring.COUNT,)), dma, dma,
            dma((Ring.COUNT,)), dma((Ring.COUNT,)), dma((Ring.COUNT,)), dma((Ring.COUNT,)),
            dma((8,)), dma((8,)), dma((18,)),
        ],
        compiler_params=pltpu.CompilerParams(
            collective_id=0, has_side_effects=True, vmem_limit_bytes=56 * 2**20
        ),
        name="gather_factor",
    )(step, working.reshape(8, B, 2048))


def split(x):
    high = x.astype(BF16)
    return high, (x - high.astype(F32)).astype(BF16)


def dot3(a, b, dims):
    dot = functools.partial(lax.dot_general, dimension_numbers=dims, preferred_element_type=F32)
    return dot(a[0], b[0]) + (dot(a[0], b[1]) + dot(a[1], b[0]))


PAIR = 2 * B
PAIRS = 8
DEPTH = 5


def update_kernel(
    step, cout, upper_any, inverse_any, rout, working, out,
    upper, inverse, columns, rows, mine, inverse_h, inverse_l, left_h, left_l, weight_h, weight_l,
    fixed_sem, rows_sem, in_sem, out_sem,
):
    k0, p, q = step[0], lax.axis_index("row"), lax.axis_index("col")
    last = k0 + STEPS - 1

    fixed = [
        pltpu.make_async_copy(inverse_any, inverse, fixed_sem.at[0]),
        pltpu.make_async_copy(upper_any, upper, fixed_sem.at[1]),
    ] + [
        pltpu.make_async_copy(cout.at[lax.rem(k0 + b, 8)], columns.at[b], fixed_sem.at[2 + b])
        for b in range(STEPS)
    ]

    def rows_in(m):
        return pltpu.make_async_copy(rout.at[pl.ds(2 * m, 2)], rows.at[m], rows_sem.at[m])

    def updated(m):
        return 2 * m * 8 + q + 8 > last

    def start(m):
        pl.when(updated(m))(rows_in(m).start)
        mine_in(m).start()

    def mine_in(m):
        here = pl.ds(pl.multiple_of(m * PAIR, PAIR), PAIR)
        return pltpu.make_async_copy(working.at[:, here], mine.at[m], in_sem.at[m])

    def mine_out(m):
        here = pl.ds(pl.multiple_of(m * PAIR, PAIR), PAIR)
        return pltpu.make_async_copy(mine.at[m], out.at[:, here], out_sem.at[m])

    for copy in fixed:
        copy.start()
    fixed[0].wait()
    for m in range(DEPTH):
        start(m)
    inverse_h[...], inverse_l[...] = split(inverse[...])
    for copy in fixed[1:]:
        copy.wait()
    for b in range(0, STEPS, 2):
        end = (b + 2) * B
        at = slice(b * B, end)
        known = split(jnp.concatenate([columns[a] for a in range(b + 2)], 1))
        x = dot3(known, (inverse_h[at, :end], inverse_l[at, :end]), NT)
        left_h[:, at], left_l[:, at] = split(x)
    for b in range(0, STEPS, 2):
        at = slice(b * B, (b + 2) * B)
        x = dot3(
            (left_h[:, b * B :], left_l[:, b * B :]),
            (inverse_h[b * B :, at], inverse_l[b * B :, at]),
            NN,
        )
        weight_h[:, at], weight_l[:, at] = split(x)

    def pair(m, carry):
        pl.when(updated(m))(rows_in(m).wait)
        mine_in(m).wait()

        @pl.when(m + DEPTH < PAIRS)
        def _():
            start(m + DEPTH)

        first = 2 * m * 8 + q

        @pl.when(updated(m))
        def _():
            x = split(jnp.concatenate([rows[m, 0], rows[m, 1]], 1))
            for part in range(4):

                @pl.when(m // 2 == part)
                def _():
                    top = part * PAIR
                    update = dot3((weight_h[top:, :], weight_l[top:, :]), x, NN)
                    for t in range(top // B, 8):
                        at = slice(t * B, (t + 1) * B)
                        for side in range(2):
                            lanes = slice(side * B, (side + 1) * B)
                            col = first + 8 * side
                            keep = (16 * t + p >= col) & (col > last)
                            part_update = update[t * B - top : (t + 1) * B - top, lanes]
                            mine[m, at, lanes] = mine[m, at, lanes] - jnp.where(
                                keep, part_update, 0.0
                            )

        for side in range(2):
            col = first + 8 * side
            lanes = slice(side * B, (side + 1) * B)

            @pl.when((col >= k0) & (col <= last))
            def _():
                b = col - k0
                at = pl.ds(pl.multiple_of(b * B, B), B)
                solved = left_h[:, at].astype(F32) + left_l[:, at].astype(F32)
                row = lax.broadcasted_iota(jnp.int32, (1024, B), 0) // B * 16 + p
                factor = jnp.concatenate([jnp.transpose(upper[b])] * 8, 0)
                mine[m, :, lanes] = jnp.where(
                    row > col, solved, jnp.where(row == col, factor, mine[m, :, lanes])
                )

        mine_out(m).start()
        return carry

    lax.fori_loop(0, PAIRS, pair, 0)
    for m in range(PAIRS):
        mine_out(m).wait()


def update_call(step, upper, inverse, rout, cout, working):
    anywhere = pl.BlockSpec(memory_space=pl.ANY)
    dma = pltpu.SemaphoreType.DMA
    return pl.pallas_call(
        update_kernel,
        out_shape=jax.ShapeDtypeStruct(working.shape, F32),
        in_specs=[pl.BlockSpec(memory_space=pltpu.SMEM)] + [anywhere] * 5,
        out_specs=anywhere,
        scratch_shapes=[
            pltpu.VMEM((STEPS, B, B), F32),
            pltpu.VMEM((W, W), F32),
            pltpu.VMEM((STEPS, 1024, B), F32),
            pltpu.VMEM((PAIRS, 2, W, B), F32),
            pltpu.VMEM((PAIRS, 1024, PAIR), F32),
            pltpu.VMEM((W, W), BF16),
            pltpu.VMEM((W, W), BF16),
            pltpu.VMEM((1024, W), BF16),
            pltpu.VMEM((1024, W), BF16),
            pltpu.VMEM((1024, W), BF16),
            pltpu.VMEM((1024, W), BF16),
            dma((8,)),
            dma((PAIRS,)),
            dma((PAIRS,)),
            dma((PAIRS,)),
        ],
        compiler_params=pltpu.CompilerParams(vmem_limit_bytes=56 * 2**20),
        name="update",
    )(step, cout, upper, inverse, rout, working)


def local(working, step):
    upper, inverse, rout, cout = gather_call(step, working)
    return update_call(step, upper, inverse, rout, cout, working)


def solution(mesh):
    placed = (P("row", "col"), P())
    return jax.shard_map(
        local, mesh=mesh, in_specs=placed, out_specs=P("row", "col"), check_vma=False
    )
```

```python
import functools

import jax
import jax.numpy as jnp
from jax import lax
from jax.experimental import pallas as pl
from jax.experimental.pallas import tpu as pltpu
from jax.sharding import PartitionSpec as P

B = 128
STEPS = 6
W = B * STEPS
LOWER = [(a, b) for a in range(STEPS) for b in range(a + 1)]
F32 = jnp.float32
BF16 = jnp.bfloat16
MESH = pl.DeviceIdType.MESH
HIGHEST = lax.Precision.HIGHEST
NT = (((1,), (1,)), ((), ()))
NN = (((1,), (0,)), ((), ()))


def factor_tile(tile, hook):
    sub = lax.broadcasted_iota(jnp.int32, (8, B), 0)
    lane = lax.broadcasted_iota(jnp.int32, (8, B), 1)
    lanes = lax.broadcasted_iota(jnp.int32, (B, B), 1)

    def spread(x, first):
        return [jnp.broadcast_to(x[:, first + i : first + i + 1], x.shape) for i in range(8)]

    head, rest = tile[:8], tile[8:]
    held = spread(head, 0)
    uppers, inverses = [], []
    for first in range(0, B, 8):
        if first == B // 2:
            hook()
        more = first + 8 < B
        if more:
            coefs = spread(rest, first)
            head_next = spread(head, first + 8)
            rest_next = spread(rest[:8], first + 8)
            at = lanes[: B - first - 8]
            rest = jnp.where((at >= first) & (at < first + 8), 0.0, rest)
        inside = (lane >= first) & (lane < first + 8)
        head = jnp.where(inside, jnp.where(lane - first == sub, 1.0, 0.0), head)
        scales = []
        for j in range(8):
            pivot = held[j][j : j + 1]
            inverse = 1.0 / pivot
            scales.append(lax.rsqrt(pivot))
            factor = jnp.where(sub > j, held[j] * inverse, 0.0)
            row = head[j : j + 1]
            cross = [held[i][j : j + 1] for i in range(8)]
            for i in range(j + 1, 8):
                held[i] = held[i] - factor * cross[i]
            if more:
                further = [head_next[i][j : j + 1] for i in range(8)]
            head = head - factor * row
            if more:
                below = coefs[j] * inverse
                for i in range(j + 1, 8):
                    coefs[i] = coefs[i] - below * cross[i]
                rest = rest - below * row
                for i in range(8):
                    head_next[i] = head_next[i] - factor * further[i]
                    rest_next[i] = rest_next[i] - below[:8] * further[i]
        scale = jnp.concatenate(scales, 0)
        done = head * scale
        upper = jnp.where(lane >= first + 8, done, 0.0)
        for i in range(8):
            upper = jnp.where((lane == first + i) & (sub <= i), held[i] * scale, upper)
        uppers.append(upper)
        inverses.append(jnp.where(lane < first + 8, done, 0.0))
        if more:
            held = rest_next
            head, rest = rest[:8], rest[8:]
    return jnp.concatenate(uppers, 0), jnp.concatenate(inverses, 0)


class Ring:
    MESSAGES = (
        (
            ((0, 0), None, (1, 0)),
            ((0, 0), None, (-1, 0)),
            ((0, 0), None, (0, 1)),
            ((0, 0), None, (0, -1)),
        ),
        (
            ((-1, 0), 0, (1, 0)),
            ((1, 0), 1, (-1, 0)),
            ((0, -1), 0, (0, 1)),
            ((0, 1), 1, (0, -1)),
            ((-1, 0), None, (0, 1)),
            ((-1, 0), None, (0, -1)),
            ((1, 0), None, (0, 1)),
            ((1, 0), None, (0, -1)),
        ),
        (
            ((2, 0), None, (0, 1)),
            ((2, 0), None, (0, -1)),
            ((-1, -1), 0, (0, 1)),
            ((1, -1), 0, (0, 1)),
            ((-1, 1), 1, (0, -1)),
            ((1, 1), 1, (0, -1)),
        ),
        (
            ((2, -1), 0, (0, 1)),
            ((2, 1), 1, (0, -1)),
        ),
    )
    COUNT = 20

    def __init__(self, row, col, view, own, send_sem, recv_sem):
        core = lax.rem(col, 2)
        x, z = row // 4, lax.rem(row, 4)
        self.u = z + core * (x - z)
        self.v = x + core * (z - x)
        self.su, self.sv = 1 + 3 * core, 4 - 3 * core
        self.col, self.view, self.own = col, view, own
        self.send_sem, self.recv_sem = send_sem, recv_sem

    def index(self, du, dv):
        return self.su * lax.rem(self.u + du + 4, 4) + self.sv * lax.rem(self.v + dv + 4, 4)

    def copy(self, number, message, receiving):
        (du, dv), part, (au, av) = message
        if receiving:
            du, dv = du - au, dv - av
        block = self.index(du, dv)
        dst = self.view(block, part)
        src = self.own if (du, dv) == (0, 0) and not receiving and self.own is not None else dst
        return pltpu.make_async_remote_copy(
            src_ref=src,
            dst_ref=dst,
            send_sem=self.send_sem.at[number],
            recv_sem=self.recv_sem.at[number],
            device_id=(self.index(au, av), self.col),
            device_id_type=MESH,
        )

    def numbered(self, tick):
        base = sum(len(m) for m in self.MESSAGES[:tick])
        return [(base + i, m) for i, m in enumerate(self.MESSAGES[tick])]

    def tick(self, tick):
        if tick > 0:
            for number, message in self.numbered(tick - 1):
                self.copy(number, message, True).wait_recv()
        if tick < len(self.MESSAGES):
            for number, message in self.numbered(tick):
                self.copy(number, message, False).start()

    def finish(self):
        for tick in range(len(self.MESSAGES)):
            for number, message in self.numbered(tick):
                self.copy(number, message, False).wait_send()


def gather_kernel(
    step_ref, working,
    upper_o, inverse_o, rout, cout,
    staged, tile, strip, slab, dbuf, dcol, dcg, dall, packed, whole, rbuf, bst,
    d1s, d1r, a1s, a1r, d2s, d2r, d3s, d3r, sibs, sibr, rs, rr, rs2, rr2, cs, cr, local,
):
    p, q = lax.axis_index("row"), lax.axis_index("col")
    core, y = lax.rem(q, 2), q // 2
    sibling = q + 1 - 2 * core
    k0 = step_ref[0]

    stages = [
        pltpu.make_async_copy(
            working.at[:, :, pl.ds(j * B, B)], staged.at[j], local.at[2 + j]
        )
        for j in range(16)
    ]
    for stage in stages:
        stage.start()
    barrier = pltpu.get_barrier_semaphore()
    for d in range(1, 16):
        pl.semaphore_signal(barrier, inc=1, device_id=(lax.rem(p + d, 16), q), device_id_type=MESH)
    for d in range(1, 8):
        pl.semaphore_signal(barrier, inc=1, device_id=(p, lax.rem(q + d, 8)), device_id_type=MESH)
    pl.semaphore_wait(barrier, 22)
    for stage in stages:
        stage.wait()

    t = jnp.minimum(lax.div(k0 + lax.rem(p - k0 + 128, 16), 16), 7)
    c = jnp.minimum(lax.div(k0 + lax.rem(q - k0 + 128, 8), 8), 15)
    tile[...] = staged[c, t]

    def remote(src, dst, send, recv, device):
        return pltpu.make_async_remote_copy(
            src_ref=src, dst_ref=dst, send_sem=send, recv_sem=recv,
            device_id=device, device_id_type=MESH,
        )

    def diag(d, slot):
        to = lax.rem(p + d, 16)
        rows = pl.ds(pl.multiple_of(8 * to, 8), 8)
        return remote(tile.at[rows, :], dbuf.at[slot], d1s.at[d], d1r.at[d], (to, q))

    def piece(d, slot):
        to = lax.rem(p + d, 16)
        return remote(strip.at[to], rbuf.at[slot], a1s.at[d], a1r.at[d], (to, q))

    def spread(d, slot):
        to = lax.rem(q + d, 8)
        return remote(dcol, dcg.at[slot], d2s.at[d], d2r.at[d], (p, to))

    for d in range(1, 16):
        diag(d, p).start()
    for j in range(16):
        strip[j] = staged[j, t]
    for d in range(1, 16):
        piece(d, p).start()
    rbuf[p] = strip[p]
    slab[...] = staged[c].reshape(1024, B)
    own_slab = pltpu.make_async_copy(slab, cout.at[q], local.at[1])
    own_slab.start()
    dbuf[p] = tile[pl.ds(pl.multiple_of(8 * p, 8), 8), :]
    for d in range(1, 16):
        diag(d, lax.rem(p + 16 - d, 16)).wait_recv()
    for s in range(STEPS):
        block = dbuf[lax.rem(k0 + s, 16)]
        dcol[s] = block
        dcg[q, s] = block
    for d in range(1, 8):
        spread(d, q).start()

    def slot(dy):
        return lax.rem(y + dy + 4, 4) * 2 + core

    def part_of(block, part):
        return cout.at[block] if part is None else cout.at[block, pl.ds(512 * part, 512), :]

    def along(n, dy, part, ay, receiving):
        block = slot(dy - ay if receiving else dy)
        dst = part_of(block, part)
        src = slab if dy == 0 and not receiving else dst
        return remote(src, dst, cs.at[n], cr.at[n], (p, slot(ay)))

    def across(n, dy, receiving):
        block = slot(dy) + 1 - 2 * core if receiving else slot(dy)
        src = slab if dy == 0 and not receiving else cout.at[block]
        return remote(src, cout.at[block], cs.at[n], cr.at[n], (p, sibling))

    along_messages = ((0, 0, None, 1), (1, 0, None, -1), (3, -1, 0, 1), (4, 1, 1, -1))
    across_messages = ((2, 0), (5, -1), (6, 1), (7, 2))

    def columns_tick(tick):
        if tick == 0:
            along(*along_messages[0], False).start()
            along(*along_messages[1], False).start()
        elif tick == 1:
            across(*across_messages[0], False).start()
            along(*along_messages[0], True).wait_recv()
            along(*along_messages[1], True).wait_recv()
            along(*along_messages[2], False).start()
            along(*along_messages[3], False).start()
            across(*across_messages[1], False).start()
            across(*across_messages[2], False).start()
        elif tick == 2:
            along(*along_messages[2], True).wait_recv()
            along(*along_messages[3], True).wait_recv()
            across(*across_messages[3], False).start()
        else:
            for message in across_messages:
                across(*message, True).wait_recv()
            for message in along_messages:
                along(*message, False).wait_send()
            for message in across_messages:
                across(*message, False).wait_send()

    for d in range(1, 8):
        spread(d, lax.rem(q + 8 - d, 8)).wait_recv()
    for n, (a, b) in enumerate(LOWER):
        dall[n] = dcg[lax.rem(k0 + b, 8), a]
    dall[len(LOWER)] = jnp.zeros((8, B), F32)
    half = pl.ds(11 * core, 11)
    packed[p, half] = dall[half]

    def block(d, slot):
        mine = packed.at[slot, half]
        return remote(mine, mine, d3s.at[d], d3r.at[d], (lax.rem(p + d, 16), q))

    def row_view(stream):
        def view(block, part):
            if part is None:
                return rout.at[block, pl.ds(384 * stream, 384), :]
            return rout.at[block, pl.ds(384 * stream + 192 * part, 192), :]

        return view

    streams = [
        Ring(p, q, row_view(0), bst.at[:384], rs, rr),
        Ring(p, q, row_view(1), bst.at[384:], rs2, rr2),
    ]
    for d in range(1, 16):
        block(d, p).start()
    columns_tick(0)

    for d in range(1, 16):
        piece(d, lax.rem(p + 16 - d, 16)).wait_recv()
    for s in range(STEPS):
        bst[s * B : (s + 1) * B, :] = rbuf[lax.rem(k0 + s, 16)]
    own_rows = pltpu.make_async_copy(bst, rout.at[p], local.at[0])
    own_rows.start()
    streams[0].tick(0)
    streams[1].tick(0)
    for d in range(1, 16):
        block(d, lax.rem(p + 16 - d, 16)).wait_recv()
    other = pl.ds(11 - 11 * core, 11)
    to_sibling = remote(packed.at[:, half], packed.at[:, half], sibs, sibr, (p, sibling))
    from_sibling = remote(packed.at[:, other], packed.at[:, other], sibs, sibr, (p, sibling))
    to_sibling.start()
    streams[0].tick(1)
    from_sibling.wait_recv()
    for n, (a, b) in enumerate(LOWER):
        whole[a, :, :, b * B : (b + 1) * B] = packed[:, n]

    def run(ring_tick, first, column_tick, second):
        ring_tick(first)
        column_tick(second)

    ticks = {
        (0, 1): lambda: run(streams[1].tick, 1, columns_tick, 1),
        (1, 1): lambda: run(streams[0].tick, 2, columns_tick, 2),
        (2, 1): lambda: streams[1].tick(2),
        (3, 1): lambda: streams[0].tick(3),
        (4, 1): lambda: streams[1].tick(3),
    }

    def tick(k, place):
        for (step, where), call in ticks.items():
            if where == place:
                pl.when(k == step)(call)

    def step(k, carry):
        here = pl.ds(pl.multiple_of(k * B, B), B)
        upper, inverse = factor_tile(
            whole[k, :, :, here].reshape(B, B), lambda: tick(k, 0)
        )
        upper_o[k] = upper
        dot = functools.partial(
            lax.dot_general, precision=HIGHEST, preferred_element_type=F32
        )
        for i in range(STEPS):

            @pl.when(k == i)
            def _():
                at = slice(i * B, (i + 1) * B)
                inverse_o[at, at] = inverse
                if i:
                    known = whole[i, :, :, : i * B].reshape(B, i * B)
                    inverse_o[at, : i * B] = dot(inverse, known, NN)
                if i < STEPS - 1:
                    left = STEPS - 1 - i
                    inverse_o[at, (i + 1) * B :] = jnp.zeros((B, left * B), F32)
                    below = whole[i + 1 :, :, :, at].reshape(left * B, B)
                    solved = dot(below, inverse, NT)
                    update = dot(solved, solved, NT)
                    whole[i + 1 :, :, :, (i + 1) * B :] = whole[
                        i + 1 :, :, :, (i + 1) * B :
                    ] - update.reshape(left, 16, 8, left * B)
                    update = dot(solved, inverse_o[at, : (i + 1) * B], NN)
                    update = update.reshape(left, 16, 8, (i + 1) * B)
                    if i:
                        whole[i + 1 :, :, :, : i * B] = (
                            whole[i + 1 :, :, :, : i * B] - update[:, :, :, : i * B]
                        )
                    whole[i + 1 :, :, :, at] = -update[:, :, :, i * B :]

        tick(k, 1)
        return carry

    lax.fori_loop(0, STEPS, step, 0)
    columns_tick(3)
    for stream in streams:
        stream.tick(4)
        stream.finish()
    to_sibling.wait_send()
    for d in range(1, 16):
        block(d, p).wait_send()
    for d in range(1, 16):
        diag(d, p).wait_send()
        piece(d, p).wait_send()
    for d in range(1, 8):
        spread(d, q).wait_send()
    own_slab.wait()
    own_rows.wait()


def gather_call(step, working):
    anywhere = pl.BlockSpec(memory_space=pl.ANY)
    vmem = pl.BlockSpec(memory_space=pltpu.VMEM)
    dma = pltpu.SemaphoreType.DMA
    return pl.pallas_call(
        gather_kernel,
        out_shape=(
            jax.ShapeDtypeStruct((STEPS, B, B), F32),
            jax.ShapeDtypeStruct((W, W), F32),
            jax.ShapeDtypeStruct((16, W, B), F32),
            jax.ShapeDtypeStruct((8, 1024, B), F32),
        ),
        in_specs=[pl.BlockSpec(memory_space=pltpu.SMEM), anywhere],
        out_specs=(vmem, vmem, anywhere, anywhere),
        scratch_shapes=[
            pltpu.VMEM((16, 8, B, B), F32),
            pltpu.VMEM((B, B), F32),
            pltpu.VMEM((16, B, B), F32),
            pltpu.VMEM((1024, B), F32),
            pltpu.VMEM((16, 8, B), F32),
            pltpu.VMEM((STEPS, 8, B), F32),
            pltpu.VMEM((8, STEPS, 8, B), F32),
            pltpu.VMEM((22, 8, B), F32),
            pltpu.VMEM((16, 22, 8, B), F32),
            pltpu.VMEM((STEPS, 16, 8, W), F32),
            pltpu.VMEM((16, B, B), F32),
            pltpu.VMEM((W, B), F32),
            dma((16,)), dma((16,)), dma((16,)), dma((16,)), dma((8,)), dma((8,)),
            dma((Ring.COUNT,)), dma((Ring.COUNT,)), dma, dma,
            dma((Ring.COUNT,)), dma((Ring.COUNT,)), dma((Ring.COUNT,)), dma((Ring.COUNT,)),
            dma((8,)), dma((8,)), dma((18,)),
        ],
        compiler_params=pltpu.CompilerParams(
            collective_id=0, has_side_effects=True, vmem_limit_bytes=56 * 2**20
        ),
        name="gather_factor",
    )(step, working.reshape(8, B, 2048))


def split(x):
    high = x.astype(BF16)
    return high, (x - high.astype(F32)).astype(BF16)


def dot3(a, b, dims):
    dot = functools.partial(lax.dot_general, dimension_numbers=dims, preferred_element_type=F32)
    return dot(a[0], b[0]) + (dot(a[0], b[1]) + dot(a[1], b[0]))


PAIR = 2 * B
PAIRS = 8
DEPTH = 5


def update_kernel(
    step, cout, upper_any, inverse_any, rout, working, out,
    upper, inverse, columns, rows, mine, inverse_h, inverse_l, left_h, left_l, weight_h, weight_l,
    fixed_sem, rows_sem, in_sem, out_sem,
):
    k0, p, q = step[0], lax.axis_index("row"), lax.axis_index("col")
    last = k0 + STEPS - 1

    fixed = [
        pltpu.make_async_copy(inverse_any, inverse, fixed_sem.at[0]),
        pltpu.make_async_copy(upper_any, upper, fixed_sem.at[1]),
    ] + [
        pltpu.make_async_copy(cout.at[lax.rem(k0 + b, 8)], columns.at[b], fixed_sem.at[2 + b])
        for b in range(STEPS)
    ]

    def rows_in(m):
        return pltpu.make_async_copy(rout.at[pl.ds(2 * m, 2)], rows.at[m], rows_sem.at[m])

    def updated(m):
        return 2 * m * 8 + q + 8 > last

    def start(m):
        pl.when(updated(m))(rows_in(m).start)
        mine_in(m).start()

    def mine_in(m):
        here = pl.ds(pl.multiple_of(m * PAIR, PAIR), PAIR)
        return pltpu.make_async_copy(working.at[:, here], mine.at[m], in_sem.at[m])

    def mine_out(m):
        here = pl.ds(pl.multiple_of(m * PAIR, PAIR), PAIR)
        return pltpu.make_async_copy(mine.at[m], out.at[:, here], out_sem.at[m])

    for copy in fixed:
        copy.start()
    fixed[0].wait()
    for m in range(DEPTH):
        start(m)
    inverse_h[...], inverse_l[...] = split(inverse[...])
    for copy in fixed[1:]:
        copy.wait()
    def panel(here):
        for b in range(0, STEPS, 2):
            end = (b + 2) * B
            at = slice(b * B, end)
            known = split(jnp.concatenate([columns[a, here] for a in range(b + 2)], 1))
            x = dot3(known, (inverse_h[at, :end], inverse_l[at, :end]), NT)
            left_h[here, at], left_l[here, at] = split(x)
        for b in range(0, STEPS, 2):
            at = slice(b * B, (b + 2) * B)
            x = dot3(
                (left_h[here, b * B :], left_l[here, b * B :]),
                (inverse_h[b * B :, at], inverse_l[b * B :, at]),
                NN,
            )
            weight_h[here, at], weight_l[here, at] = split(x)

    for n in range(2):
        size = 1024 // 2
        bottom = (n + 1) * size // B - 1
        pl.when(16 * bottom + p > k0)(functools.partial(panel, slice(n * size, (n + 1) * size)))

    def pair(m, carry):
        pl.when(updated(m))(rows_in(m).wait)
        mine_in(m).wait()

        @pl.when(m + DEPTH < PAIRS)
        def _():
            start(m + DEPTH)

        first = 2 * m * 8 + q

        @pl.when(updated(m))
        def _():
            x = split(jnp.concatenate([rows[m, 0], rows[m, 1]], 1))
            for part in range(4):

                @pl.when(m // 2 == part)
                def _():
                    top = part * PAIR
                    update = dot3((weight_h[top:, :], weight_l[top:, :]), x, NN)
                    for t in range(top // B, 8):
                        at = slice(t * B, (t + 1) * B)
                        for side in range(2):
                            lanes = slice(side * B, (side + 1) * B)
                            col = first + 8 * side
                            keep = (16 * t + p >= col) & (col > last)
                            part_update = update[t * B - top : (t + 1) * B - top, lanes]
                            mine[m, at, lanes] = mine[m, at, lanes] - jnp.where(
                                keep, part_update, 0.0
                            )

        for side in range(2):
            col = first + 8 * side
            lanes = slice(side * B, (side + 1) * B)

            @pl.when((col >= k0) & (col <= last))
            def _():
                b = col - k0
                at = pl.ds(pl.multiple_of(b * B, B), B)
                solved = left_h[:, at].astype(F32) + left_l[:, at].astype(F32)
                row = lax.broadcasted_iota(jnp.int32, (1024, B), 0) // B * 16 + p
                factor = jnp.concatenate([jnp.transpose(upper[b])] * 8, 0)
                mine[m, :, lanes] = jnp.where(
                    row > col, solved, jnp.where(row == col, factor, mine[m, :, lanes])
                )

        mine_out(m).start()
        return carry

    lax.fori_loop(0, PAIRS, pair, 0)
    for m in range(PAIRS):
        mine_out(m).wait()


def update_call(step, upper, inverse, rout, cout, working):
    anywhere = pl.BlockSpec(memory_space=pl.ANY)
    dma = pltpu.SemaphoreType.DMA
    return pl.pallas_call(
        update_kernel,
        out_shape=jax.ShapeDtypeStruct(working.shape, F32),
        in_specs=[pl.BlockSpec(memory_space=pltpu.SMEM)] + [anywhere] * 5,
        out_specs=anywhere,
        scratch_shapes=[
            pltpu.VMEM((STEPS, B, B), F32),
            pltpu.VMEM((W, W), F32),
            pltpu.VMEM((STEPS, 1024, B), F32),
            pltpu.VMEM((PAIRS, 2, W, B), F32),
            pltpu.VMEM((PAIRS, 1024, PAIR), F32),
            pltpu.VMEM((W, W), BF16),
            pltpu.VMEM((W, W), BF16),
            pltpu.VMEM((1024, W), BF16),
            pltpu.VMEM((1024, W), BF16),
            pltpu.VMEM((1024, W), BF16),
            pltpu.VMEM((1024, W), BF16),
            dma((8,)),
            dma((PAIRS,)),
            dma((PAIRS,)),
            dma((PAIRS,)),
        ],
        compiler_params=pltpu.CompilerParams(vmem_limit_bytes=56 * 2**20),
        name="update",
    )(step, cout, upper, inverse, rout, working)


def local(working, step):
    upper, inverse, rout, cout = gather_call(step, working)
    return update_call(step, upper, inverse, rout, cout, working)


def solution(mesh):
    placed = (P("row", "col"), P())
    return jax.shard_map(
        local, mesh=mesh, in_specs=placed, out_specs=P("row", "col"), check_vma=False
    )
```
